256 devices in a mesh: polar: 32 (over z_hi, y, x), azimuth: 8 (over z_lo, core).
Axes of the slice: x: 4, y: 4, z: 8 (z_hi: 2, z_lo: 4; z = z_hi * 4 + z_lo), core: 2. Of those that a mesh axis runs over, the one named last changes fastest.
Arguments:
- features: bfloat16 [256, 1440, 256], P('polar', 'azimuth'), may hold values from -6 to 6
- cotangent: bfloat16 [256, 1440, 256], P('polar', 'azimuth'), may hold values from -6 to 6
- mixing: bfloat16 [256, 9, 256], replicated, may hold values from -0.125 to 0.125
- response: bfloat16 [9, 256, 9, 2, 720], P(None, 'polar', None, None, 'azimuth'), may hold values from -1.5 to 1.5
- offsets: int32 [256], P('polar'), may hold values from 0 to 247, as said below
Outputs:
- grad_features: bfloat16 [256, 1440, 256], P('polar', 'azimuth')
- grad_mixing: float32 [256, 9, 256], P('azimuth')
The draws below stay inside these ranges and needn't reach their ends.
Inputs may be any that keep to these rules, and one draw needn't show every extreme that they name: offsets[l] lies from l - 8 up to l + 9 - 9 (that is l itself), clipped to 0 .. 247; in every aligned block of 8 rows one row takes each end of that range.
All inputs are finite; a program needn't handle non-finite values.
Results may differ from the reference program's by a relative error of at most 0.012.
Values may be sent and summed in bfloat16 or wider, within the bound.
No kernel may reach another device: no remote copies, remote signals or barrier semaphores. Data moves between devices by JAX's collectives and lax.ppermute only.
A program may use at most 128 MiB of HBM per device.

```python
import math
import jax
import jax.numpy as jnp
from jax import lax

C = 256
K = 9
NLON = 1440
NM = 720
LAT_DEV = 8
HALO = 8
BW = 9
NLAT = 256


def draw_offsets(key, part):
    row_index = jnp.arange(NLAT, dtype=jnp.int32)
    span_count = 2 * HALO - BW + 2
    key_first, key_second, key_third = jax.random.split(key, 3)
    step_draw = jax.random.randint(key_first, (NLAT,), 0, span_count, dtype=jnp.int32)
    block_count = NLAT // LAT_DEV
    low_place = jax.random.randint(key_second, (block_count,), 0, LAT_DEV, dtype=jnp.int32)
    gap_draw = jax.random.randint(key_third, (block_count,), 1, LAT_DEV, dtype=jnp.int32)
    high_place = (low_place + gap_draw) % LAT_DEV
    within_block = row_index % LAT_DEV
    block_index = row_index // LAT_DEV
    step_draw = jnp.where(within_block == low_place[block_index], 0, step_draw)
    step_draw = jnp.where(within_block == high_place[block_index], span_count - 1, step_draw)
    return jnp.clip(row_index - HALO + step_draw, 0, NLAT - BW).astype(jnp.int32)


def block_levels(key, extent, cuts, least, largest):
    level = 1.0
    for dim, parts in cuts:
        heights = jax.random.uniform(jax.random.fold_in(jax.random.fold_in(key, 6), dim), (parts,), jnp.float32, least / len(cuts), largest / len(cuts))
        level = level * jnp.repeat(jnp.exp(heights), extent[dim] // parts).reshape((-1,) + (1,) * (len(extent) - 1 - dim))
    return level


def scatter_about(rng, dims, scale, limit, pieces=(), kind=jnp.bfloat16):
    drawn = jax.random.normal(rng, dims, jnp.float32) * scale
    if len(pieces) > 0:
        drawn = block_levels(rng, dims, pieces, -0.22, 0.18) * drawn
    return jnp.clip(drawn, min=-limit, max=limit).astype(kind)


def setup_inputs(seed: int = 0) -> dict:
    arg_keys = jax.random.split(jax.random.key(seed), 6)
    return {
        "features": scatter_about(arg_keys[0], (NLAT, NLON, C), 1.0, 6.0, ((0, 32), (1, 8))),
        "cotangent": scatter_about(arg_keys[1], (NLAT, NLON, C), 1.0, 6.0, ((0, 32), (1, 8))),
        "mixing": scatter_about(arg_keys[2], (C, K, C), (K * C) ** -0.5, 0.125),
        "response": scatter_about(arg_keys[3], (K, NLAT, BW, 2, NM), (2 * BW) ** -0.5, 1.5, ((1, 32), (4, 8))),
        "offsets": draw_offsets(jax.random.fold_in(arg_keys[5], 71), 0),
    }


def transform_table(nlon, nmodes):
    mode_index = jnp.arange(nmodes, dtype=jnp.int32)[:, None]
    cell_index = jnp.arange(nlon, dtype=jnp.int32)[None, :]
    phases = mode_index * cell_index % nlon
    angles = phases.astype(jnp.float32) * (2.0 * math.pi / nlon)
    norm_scale = 1.0 / math.sqrt(nlon)
    return jnp.stack((jnp.cos(angles) * norm_scale, -jnp.sin(angles) * norm_scale))

def reference(features, cotangent, mixing, response, offsets):
    base_table = transform_table(NLON, NM)
    mode_index = jnp.arange(NM, dtype=jnp.int32)
    mode_weight = jnp.where(mode_index == 0, 1.0, 2.0).astype(jnp.float32)
    forward = base_table.astype(jnp.bfloat16)
    weighted = (base_table * mode_weight[None, :, None]).astype(jnp.bfloat16)
    fwd_wide = forward.astype(jnp.float32)
    wgt_wide = weighted.astype(jnp.float32)

    def analyse_row(pair):
        feat_row, cot_row = pair
        spec_row = jnp.einsum('pmn,nc->pmc', fwd_wide, feat_row.astype(jnp.float32), precision=lax.Precision.HIGHEST).astype(jnp.bfloat16)
        cospec_row = jnp.einsum('pmn,nc->pmc', wgt_wide, cot_row.astype(jnp.float32), precision=lax.Precision.HIGHEST).astype(jnp.bfloat16)
        return (spec_row, cospec_row)
    spectra, cospectra = lax.map(analyse_row, (features, cotangent))
    spectra = lax.optimization_barrier(spectra)
    spec_wide = spectra.astype(jnp.float32)
    flat_co = cospectra.reshape(NLAT * 2 * NM, C)
    mix_basis = jnp.moveaxis(mixing, 1, 0)

    def per_basis(dual_sum, basis_item):
        resp_k, weight_k = basis_item

        def forward_step(band_step, outs):
            out_re, out_im = outs
            band_rows = (offsets + band_step).astype(jnp.int32)
            picked = spec_wide[band_rows]
            resp_j = lax.dynamic_index_in_dim(resp_k, band_step, 1, False).astype(jnp.float32)
            resp_re = resp_j[:, 0, :][:, :, None]
            resp_im = resp_j[:, 1, :][:, :, None]
            out_re = out_re + resp_re * picked[:, 0] - resp_im * picked[:, 1]
            out_im = out_im + resp_re * picked[:, 1] + resp_im * picked[:, 0]
            return (out_re, out_im)
        zero_out = jnp.zeros((NLAT, NM, C), jnp.float32)
        out_re, out_im = lax.fori_loop(0, BW, forward_step, (zero_out, zero_out))
        mixed_k = jnp.stack((out_re, out_im), 1).astype(jnp.bfloat16)
        grad_k = jnp.dot(flat_co.T, mixed_k.reshape(NLAT * 2 * NM, C), preferred_element_type=jnp.float32)
        dual_k = jnp.dot(flat_co, weight_k, preferred_element_type=jnp.float32).astype(jnp.bfloat16)
        dual_k = lax.optimization_barrier(dual_k)
        dual_wide = dual_k.astype(jnp.float32).reshape(NLAT, 2, NM, C)

        def adjoint_step(band_step, running):
            band_rows = (offsets + band_step).astype(jnp.int32)
            resp_j = lax.dynamic_index_in_dim(resp_k, band_step, 1, False).astype(jnp.float32)
            resp_re = resp_j[:, 0, :][:, :, None]
            resp_im = resp_j[:, 1, :][:, :, None]
            add_re = resp_re * dual_wide[:, 0] + resp_im * dual_wide[:, 1]
            add_im = resp_re * dual_wide[:, 1] - resp_im * dual_wide[:, 0]
            return running.at[band_rows].add(jnp.stack((add_re, add_im), 1))
        dual_sum = lax.fori_loop(0, BW, adjoint_step, dual_sum)
        return (dual_sum, grad_k)
    initial = jnp.zeros((NLAT, 2, NM, C), jnp.float32)
    dual_sum, grad_stack = lax.scan(per_basis, initial, (response, mix_basis))
    grad_mixing = jnp.moveaxis(grad_stack, 0, 1) * (1.0 / math.sqrt(NLAT * NLON))
    dual_spectra = dual_sum.astype(jnp.bfloat16)
    dual_spectra = lax.optimization_barrier(dual_spectra)

    def synthesise_row(dual_row):
        return jnp.einsum('pmn,pmc->nc', fwd_wide, dual_row.astype(jnp.float32), precision=lax.Precision.HIGHEST).astype(jnp.bfloat16)
    grad_features = lax.map(synthesise_row, dual_spectra)
    return (grad_features, grad_mixing)
```

```python
import math

import jax
import jax.numpy as jnp
from jax import lax
from jax.experimental import pallas as pl
from jax.experimental.pallas import tpu as pltpu
from jax.sharding import Mesh
from jax.sharding import PartitionSpec as P

BF = jnp.bfloat16
F32 = jnp.float32

K = 9
BW = 9
C = 256
NLON = 1440
NM = 720
REACH = 8
GRP = 32
TM = 24
GM = 90
MB = 4

ROWS_AX = ("zh", "y")
MODE_AX = ("x", "zl", "co")
AZ_AX = ("zl", "co")


def mode_table():
    n = jnp.arange(NLON, dtype=jnp.int32)
    xq = jnp.arange(4, dtype=jnp.int32)
    g = jnp.arange(8, dtype=jnp.int32)
    first = (xq[:, None] * TM + g[None, :] * GM).reshape(32)
    t = jnp.arange(TM, dtype=jnp.int32)
    step = 2.0 * math.pi / NLON
    ang_a = (first[:, None] * n[None, :] % NLON).astype(F32) * step
    ang_b = (t[:, None] * n[None, :] % NLON).astype(F32) * step
    norm = 1.0 / math.sqrt(NLON)
    ca, sa = jnp.cos(ang_a) * norm, jnp.sin(ang_a) * norm
    cb, sb = jnp.cos(ang_b), jnp.sin(ang_b)
    ca, sa, cb, sb = lax.optimization_barrier((ca, sa, cb, sb))
    ca, sa = ca[:, None, :], sa[:, None, :]
    cb, sb = cb[None], sb[None]
    real = (xq[:, None, None] * TM + t[None, None, :] < GM) & (g[None, :, None] >= 0)
    real = real.reshape(32, TM)[:, :, None].astype(F32)
    table = jnp.stack(((ca * cb - sa * sb) * real, -(sa * cb + ca * sb) * real), axis=1)
    return table.astype(BF).reshape(32 * 2 * TM, NLON)


def shift(x, axis, by):
    length = lax.axis_size(axis)
    return lax.ppermute(x, axis, [(i, i + by) for i in range(length) if 0 <= i + by < length])


def ring_pieces(x, axis):
    n = lax.axis_size(axis)
    me = lax.axis_index(axis)
    own = lax.dynamic_index_in_dim(x, me, 0, False)
    got = []
    for s in range(1, n):
        piece = lax.dynamic_index_in_dim(x, lax.rem(me + s, n), 0, False)
        got.append((s, lax.ppermute(piece, axis, [(i, (i + s) % n) for i in range(n)])))
    return own, got


def ring_exchange(x, axis):
    n = lax.axis_size(axis)
    me = lax.axis_index(axis)
    own, got = ring_pieces(x, axis)
    out = lax.dynamic_update_index_in_dim(jnp.zeros_like(x), own, me, 0)
    for s, piece in got:
        out = lax.dynamic_update_index_in_dim(out, piece, lax.rem(me + n - s, n), 0)
    return out


def ring_sum(x, axis):
    own, got = ring_pieces(x.astype(BF), axis)
    total = own.astype(F32)
    for _, piece in got:
        total = total + piece.astype(F32)
    return total


def ring_gather(x, axis):
    n = lax.axis_size(axis)
    me = lax.axis_index(axis)
    out = lax.dynamic_update_index_in_dim(jnp.zeros((n,) + x.shape, x.dtype), x, me, 0)
    for s in range(1, n):
        piece = lax.ppermute(x, axis, [(i, (i + s) % n) for i in range(n)])
        out = lax.dynamic_update_index_in_dim(out, piece, lax.rem(me + n - s, n), 0)
    return out


def band_matrices(response, offsets):
    first = (lax.axis_index("zh") * 4 + lax.axis_index("y")) * GRP + lax.axis_index("x") * 8
    rel = (offsets - first - jnp.arange(8, dtype=jnp.int32)).astype(BF)
    flat = jnp.transpose(response, (4, 1, 0, 2, 3)).reshape(GM, 8, K * BW * 2)
    flat = jnp.pad(flat, ((0, 4 * TM - GM), (0, 0), (0, 0)))
    flat = jnp.concatenate((flat, jnp.broadcast_to(rel[None, :, None], (4 * TM, 8, 1))), axis=2)
    wide = K * BW * 2 + 1
    parts = ring_exchange(flat.reshape(4, TM, 8 * wide), "x")
    low = shift(parts[3], ROWS_AX, 1)
    high = shift(parts[0], ROWS_AX, -1)
    parts = parts.reshape(4, TM, 8, wide)
    own = jnp.transpose(parts, (1, 3, 0, 2)).reshape(TM, wide, GRP)
    halo = jnp.transpose(jnp.stack((low, high), 0).reshape(2, TM, 8, wide), (1, 3, 0, 2))
    halo = halo.reshape(TM, wide, 2 * REACH)

    def columns(v):
        resp = v[:, :-1].astype(F32).reshape(TM, K, BW, 2, v.shape[2])
        a, b = resp[:, :, :, 0], resp[:, :, :, 1]
        return jnp.stack((jnp.concatenate((a, b), -1), jnp.concatenate((-b, a), -1)), 3)

    value = jnp.concatenate((columns(own), columns(halo)), -1)
    place_own = own[0, -1].astype(jnp.int32) + jnp.arange(GRP, dtype=jnp.int32)
    rim = jnp.arange(REACH, dtype=jnp.int32)
    place_halo = halo[0, -1].astype(jnp.int32) + jnp.concatenate((rim - REACH, rim + GRP))
    place = jnp.concatenate((place_own, place_own, place_halo, place_halo))
    which = jnp.arange(GRP, dtype=jnp.int32)[:, None] - place[None, :]
    value = lax.optimization_barrier(value)
    dense = jnp.zeros((TM, K, 2, GRP, 96), F32)
    for j in range(BW):
        dense = jnp.where(which == j, value[:, :, j, :, None, :], dense)
    return dense.astype(BF).reshape(TM, K * 2 * GRP, 96)


def dual_kernel(band_ref, own_ref, halo_ref, mix_ref, z_ref, dual_ref, column_ref):
    for m in range(MB):
        column_ref[0:64, :] = own_ref[m]
        column_ref[64:96, :] = halo_ref[m]
        z = jnp.dot(band_ref[m], column_ref[...], preferred_element_type=F32).astype(BF)
        for k in range(K):
            z_ref[k, m] = z[k * 64 : (k + 1) * 64]
    total = jnp.zeros((MB * 64, C), F32)
    for k in range(K):
        total = total + jnp.dot(
            z_ref[k].reshape(MB * 64, C), mix_ref[k], preferred_element_type=F32
        )
    dual_ref[...] = total.astype(BF).reshape(MB, 64, C)


def dual_call(band, own, halo, mix):
    return pl.pallas_call(
        dual_kernel,
        grid=(TM // MB,),
        in_specs=[
            pl.BlockSpec((MB, K * 64, 96), lambda i: (i, 0, 0)),
            pl.BlockSpec((MB, 64, C), lambda i: (i, 0, 0)),
            pl.BlockSpec((MB, 32, C), lambda i: (i, 0, 0)),
            pl.BlockSpec((K, C, C), lambda i: (0, 0, 0)),
        ],
        out_specs=[
            pl.BlockSpec((K, MB, 64, C), lambda i: (0, i, 0, 0)),
            pl.BlockSpec((MB, 64, C), lambda i: (i, 0, 0)),
        ],
        out_shape=[
            jax.ShapeDtypeStruct((K, TM, 64, C), BF),
            jax.ShapeDtypeStruct((TM, 64, C), BF),
        ],
        scratch_shapes=[pltpu.VMEM((96, C), BF)],
        compiler_params=pltpu.CompilerParams(vmem_limit_bytes=40 * 1024 * 1024),
        cost_estimate=pl.CostEstimate(
            flops=2 * TM * 576 * C * 96 + 2 * TM * 64 * K * C * C,
            bytes_accessed=16_000_000,
            transcendentals=0,
        ),
    )(band, own, halo, mix)


def to_modes(spec):
    return lax.all_to_all(spec.reshape(32, 2 * TM, C), MODE_AX, 0, 0, tiled=True)


def by_mode(block):
    rows = block.shape[0]
    return jnp.transpose(block.reshape(rows, 2, TM, C), (2, 1, 0, 3))


def per_device(features, cotangent, mixing, response, offsets):
    cot_row = lax.all_to_all(cotangent, AZ_AX, 0, 0, tiled=True).reshape(NLON, C)
    table = mode_table()
    mix_basis = jnp.moveaxis(mixing, 1, 0)
    band = band_matrices(response, offsets)
    feat_row = lax.all_to_all(features, AZ_AX, 0, 0, tiled=True).reshape(NLON, C)

    q = jnp.arange(32 * 2 * TM, dtype=jnp.int32)
    first_mode = (q // (2 * TM) == 0) & (q % TM == 0)
    weight = jnp.where(first_mode, 1.0, 2.0).astype(F32)[:, None]
    cospec = (jnp.dot(table, cot_row, preferred_element_type=F32) * weight).astype(BF)
    cospec = to_modes(cospec)
    low = shift(cospec[GRP - REACH :], ROWS_AX, 1)
    high = shift(cospec[:REACH], ROWS_AX, -1)
    own = by_mode(cospec).reshape(TM, 64, C)
    halo = by_mode(jnp.concatenate((low, high), 0)).reshape(TM, 32, C)

    spec = jnp.dot(table, feat_row, preferred_element_type=F32).astype(BF)
    spec = by_mode(to_modes(spec)).reshape(TM * 64, C)

    z, dual = dual_call(band, own, halo, mix_basis)

    dual = jnp.transpose(dual.reshape(TM, 2, GRP, C), (2, 1, 0, 3)).reshape(GRP, 2 * TM, C)
    dual_row = lax.all_to_all(dual, MODE_AX, 0, 0, tiled=True).reshape(32 * 2 * TM, C)
    cells = lax.dot_general(
        table, dual_row, (((0,), (0,)), ((), ())), preferred_element_type=F32
    ).astype(BF)
    grad_features = lax.all_to_all(cells.reshape(8, NLON // 8, C), AZ_AX, 0, 0, tiled=True)

    grad = jnp.einsum(
        "kno,ni->koi", z.reshape(K, TM * 64, C), spec, preferred_element_type=F32
    )
    grad = jnp.transpose(grad.reshape(K, 8, 32, C), (1, 0, 2, 3)).reshape(8, 4, 4, 18, C)
    grad = jnp.transpose(grad, (1, 2, 0, 3, 4)).astype(BF)
    grad = ring_sum(grad, "x")
    grad = ring_sum(grad, "y")
    grad = ring_sum(grad.reshape(4, 2, 18, C), "zl")
    grad = ring_sum(grad, "co")
    grad = grad + lax.ppermute(grad, "zh", [(0, 1), (1, 0)])
    grad = grad * (1.0 / math.sqrt(256 * NLON))
    grad = ring_gather(ring_gather(grad, "y"), "x")
    grad_mixing = jnp.transpose(grad.reshape(K, 32, C), (1, 0, 2))
    return grad_features, grad_mixing


def solution(mesh):
    fine = Mesh(mesh.devices.reshape(2, 4, 4, 4, 2), ("zh", "y", "x", "zl", "co"))
    rows = ("zh", "y", "x")
    return jax.shard_map(
        per_device,
        mesh=fine,
        in_specs=(
            P(rows, AZ_AX, None),
            P(rows, AZ_AX, None),
            P(),
            P(None, rows, None, None, AZ_AX),
            P(rows),
        ),
        out_specs=(P(rows, AZ_AX, None), P(AZ_AX, None, None)),
        check_vma=False,
    )
```

```python
import math

import jax
import jax.numpy as jnp
from jax import lax
from jax.experimental import pallas as pl
from jax.experimental.pallas import tpu as pltpu
from jax.sharding import Mesh
from jax.sharding import PartitionSpec as P

BF = jnp.bfloat16
F32 = jnp.float32

K = 9
BW = 9
C = 256
NLON = 1440
NM = 720
REACH = 8
GRP = 32
TM = 24
GM = 90
MB = 4

ROWS_AX = ("zh", "y")
MODE_AX = ("x", "zl", "co")
AZ_AX = ("zl", "co")


def mode_table():
    n = jnp.arange(NLON, dtype=jnp.int32)
    xq = jnp.arange(4, dtype=jnp.int32)
    g = jnp.arange(8, dtype=jnp.int32)
    first = (xq[:, None] * TM + g[None, :] * GM).reshape(32)
    t = jnp.arange(TM, dtype=jnp.int32)
    step = 2.0 * math.pi / NLON
    ang_a = (first[:, None] * n[None, :] % NLON).astype(F32) * step
    ang_b = (t[:, None] * n[None, :] % NLON).astype(F32) * step
    norm = 1.0 / math.sqrt(NLON)
    ca, sa = jnp.cos(ang_a) * norm, jnp.sin(ang_a) * norm
    cb, sb = jnp.cos(ang_b), jnp.sin(ang_b)
    ca, sa, cb, sb = lax.optimization_barrier((ca, sa, cb, sb))
    ca, sa = ca[:, None, :], sa[:, None, :]
    cb, sb = cb[None], sb[None]
    real = (xq[:, None, None] * TM + t[None, None, :] < GM) & (g[None, :, None] >= 0)
    real = real.reshape(32, TM)[:, :, None].astype(F32)
    table = jnp.stack(((ca * cb - sa * sb) * real, -(sa * cb + ca * sb) * real), axis=1)
    return table.astype(BF).reshape(32 * 2 * TM, NLON)


def shift(x, axis, by):
    length = lax.axis_size(axis)
    return lax.ppermute(x, axis, [(i, i + by) for i in range(length) if 0 <= i + by < length])


def ring_pieces(x, axis):
    n = lax.axis_size(axis)
    me = lax.axis_index(axis)
    own = lax.dynamic_index_in_dim(x, me, 0, False)
    got = []
    for s in range(1, n):
        piece = lax.dynamic_index_in_dim(x, lax.rem(me + s, n), 0, False)
        got.append((s, lax.ppermute(piece, axis, [(i, (i + s) % n) for i in range(n)])))
    return own, got


def ring_exchange(x, axis):
    n = lax.axis_size(axis)
    me = lax.axis_index(axis)
    own, got = ring_pieces(x, axis)
    out = lax.dynamic_update_index_in_dim(jnp.zeros_like(x), own, me, 0)
    for s, piece in got:
        out = lax.dynamic_update_index_in_dim(out, piece, lax.rem(me + n - s, n), 0)
    return out


def ring_sum(x, axis):
    own, got = ring_pieces(x.astype(BF), axis)
    total = own.astype(F32)
    for _, piece in got:
        total = total + piece.astype(F32)
    return total


def ring_gather(x, axis):
    n = lax.axis_size(axis)
    me = lax.axis_index(axis)
    out = lax.dynamic_update_index_in_dim(jnp.zeros((n,) + x.shape, x.dtype), x, me, 0)
    for s in range(1, n):
        piece = lax.ppermute(x, axis, [(i, (i + s) % n) for i in range(n)])
        out = lax.dynamic_update_index_in_dim(out, piece, lax.rem(me + n - s, n), 0)
    return out


def band_matrices(response, offsets):
    first = (lax.axis_index("zh") * 4 + lax.axis_index("y")) * GRP + lax.axis_index("x") * 8
    rel = (offsets - first - jnp.arange(8, dtype=jnp.int32)).astype(BF)
    flat = jnp.transpose(response, (4, 1, 0, 2, 3)).reshape(GM, 8, K * BW * 2)
    flat = jnp.pad(flat, ((0, 4 * TM - GM), (0, 0), (0, 0)))
    flat = jnp.concatenate((flat, jnp.broadcast_to(rel[None, :, None], (4 * TM, 8, 1))), axis=2)
    wide = K * BW * 2 + 1
    parts = ring_exchange(flat.reshape(4, TM, 8 * wide), "x")
    low = shift(parts[3], ROWS_AX, 1)
    high = shift(parts[0], ROWS_AX, -1)
    parts = parts.reshape(4, TM, 8, wide)
    own = jnp.transpose(parts, (1, 3, 0, 2)).reshape(TM, wide, GRP)
    halo = jnp.transpose(jnp.stack((low, high), 0).reshape(2, TM, 8, wide), (1, 3, 0, 2))
    halo = halo.reshape(TM, wide, 2 * REACH)

    def columns(v):
        resp = v[:, :-1].astype(F32).reshape(TM, K, BW, 2, v.shape[2])
        a, b = resp[:, :, :, 0], resp[:, :, :, 1]
        return jnp.stack((jnp.concatenate((a, b), -1), jnp.concatenate((-b, a), -1)), 3)

    value = jnp.concatenate((columns(own), columns(halo)), -1)
    place_own = own[0, -1].astype(jnp.int32) + jnp.arange(GRP, dtype=jnp.int32)
    rim = jnp.arange(REACH, dtype=jnp.int32)
    place_halo = halo[0, -1].astype(jnp.int32) + jnp.concatenate((rim - REACH, rim + GRP))
    place = jnp.concatenate((place_own, place_own, place_halo, place_halo))
    which = jnp.arange(GRP, dtype=jnp.int32)[:, None] - place[None, :]
    value = lax.optimization_barrier(value)
    dense = jnp.zeros((TM, K, 2, GRP, 96), F32)
    for j in range(BW):
        dense = jnp.where(which == j, value[:, :, j, :, None, :], dense)
    return dense.astype(BF).reshape(TM, K * 2 * GRP, 96)


def dual_kernel(band_ref, own_ref, halo_ref, mix_ref, z_ref, dual_ref, column_ref):
    for m in range(MB):
        column_ref[0:64, :] = own_ref[m]
        column_ref[64:96, :] = halo_ref[m]
        z = jnp.dot(band_ref[m], column_ref[...], preferred_element_type=F32).astype(BF)
        for k in range(K):
            z_ref[k, m] = z[k * 64 : (k + 1) * 64]
    total = jnp.zeros((MB * 64, C), F32)
    for k in range(K):
        total = total + jnp.dot(
            z_ref[k].reshape(MB * 64, C), mix_ref[k], preferred_element_type=F32
        )
    dual_ref[...] = total.astype(BF).reshape(MB, 64, C)


def dual_call(band, own, halo, mix):
    return pl.pallas_call(
        dual_kernel,
        grid=(TM // MB,),
        in_specs=[
            pl.BlockSpec((MB, K * 64, 96), lambda i: (i, 0, 0)),
            pl.BlockSpec((MB, 64, C), lambda i: (i, 0, 0)),
            pl.BlockSpec((MB, 32, C), lambda i: (i, 0, 0)),
            pl.BlockSpec((K, C, C), lambda i: (0, 0, 0)),
        ],
        out_specs=[
            pl.BlockSpec((K, MB, 64, C), lambda i: (0, i, 0, 0)),
            pl.BlockSpec((MB, 64, C), lambda i: (i, 0, 0)),
        ],
        out_shape=[
            jax.ShapeDtypeStruct((K, TM, 64, C), BF),
            jax.ShapeDtypeStruct((TM, 64, C), BF),
        ],
        scratch_shapes=[pltpu.VMEM((96, C), BF)],
        compiler_params=pltpu.CompilerParams(vmem_limit_bytes=40 * 1024 * 1024),
        cost_estimate=pl.CostEstimate(
            flops=2 * TM * 576 * C * 96 + 2 * TM * 64 * K * C * C,
            bytes_accessed=16_000_000,
            transcendentals=0,
        ),
    )(band, own, halo, mix)


def grad_kernel(spec_ref, z_ref, out_ref, turned_ref):
    @pl.when(pl.program_id(0) == 0)
    def _():
        turned_ref[...] = spec_ref[...].T

    product = jnp.dot(turned_ref[...], z_ref[0], preferred_element_type=F32)
    out_ref[...] = product.T.astype(BF).reshape(8, 1, 32, C)


def grad_call(spec, z):
    return pl.pallas_call(
        grad_kernel,
        grid=(K,),
        in_specs=[
            pl.BlockSpec((TM * 64, C), lambda k: (0, 0)),
            pl.BlockSpec((1, TM * 64, C), lambda k: (k, 0, 0)),
        ],
        out_specs=pl.BlockSpec((8, 1, 32, C), lambda k: (0, k, 0, 0)),
        out_shape=jax.ShapeDtypeStruct((8, K, 32, C), BF),
        scratch_shapes=[pltpu.VMEM((C, TM * 64), BF)],
        compiler_params=pltpu.CompilerParams(vmem_limit_bytes=24 * 1024 * 1024),
        cost_estimate=pl.CostEstimate(
            flops=2 * TM * 64 * K * C * C, bytes_accessed=9_000_000, transcendentals=0
        ),
    )(spec, z)


def to_modes(spec):
    return lax.all_to_all(spec.reshape(32, 2 * TM, C), MODE_AX, 0, 0, tiled=True)


def by_mode(block):
    rows = block.shape[0]
    return jnp.transpose(block.reshape(rows, 2, TM, C), (2, 1, 0, 3))


def per_device(features, cotangent, mixing, response, offsets):
    cot_row = lax.all_to_all(cotangent, AZ_AX, 0, 0, tiled=True).reshape(NLON, C)
    table = mode_table()
    mix_basis = jnp.moveaxis(mixing, 1, 0)
    cot_row, response, offsets = lax.optimization_barrier((cot_row, response, offsets))
    band = band_matrices(response, offsets)
    feat_row = lax.all_to_all(features, AZ_AX, 0, 0, tiled=True).reshape(NLON, C)

    q = jnp.arange(32 * 2 * TM, dtype=jnp.int32)
    first_mode = (q // (2 * TM) == 0) & (q % TM == 0)
    weight = jnp.where(first_mode, 1.0, 2.0).astype(F32)[:, None]
    cospec = (jnp.dot(table, cot_row, preferred_element_type=F32) * weight).astype(BF)
    cospec = to_modes(cospec)
    low = shift(cospec[GRP - REACH :], ROWS_AX, 1)
    high = shift(cospec[:REACH], ROWS_AX, -1)
    own = by_mode(cospec).reshape(TM, 64, C)
    halo = by_mode(jnp.concatenate((low, high), 0)).reshape(TM, 32, C)

    spec = jnp.dot(table, feat_row, preferred_element_type=F32).astype(BF)
    spec = by_mode(to_modes(spec)).reshape(TM * 64, C)

    z, dual = dual_call(band, own, halo, mix_basis)

    dual = jnp.transpose(dual.reshape(TM, 2, GRP, C), (2, 1, 0, 3)).reshape(GRP, 2 * TM, C)
    dual_row = lax.all_to_all(dual, MODE_AX, 0, 0, tiled=True).reshape(32 * 2 * TM, C)
    grad = grad_call(spec, z.reshape(K, TM * 64, C)).reshape(8, 4, 72, C)
    grad = ring_sum(jnp.moveaxis(grad, 1, 0), "x").astype(BF)
    grad, dual_row = lax.optimization_barrier((grad, dual_row))
    cells = lax.dot_general(
        table, dual_row, (((0,), (0,)), ((), ())), preferred_element_type=F32
    ).astype(BF)
    grad_features = lax.all_to_all(cells.reshape(8, NLON // 8, C), AZ_AX, 0, 0, tiled=True)

    grad = ring_sum(jnp.moveaxis(grad.reshape(8, 4, 18, C), 1, 0), "y")
    grad = ring_sum(grad.reshape(4, 2, 18, C), "zl")
    grad = ring_sum(grad, "co")
    grad = grad + lax.ppermute(grad, "zh", [(0, 1), (1, 0)])
    grad = grad * (1.0 / math.sqrt(256 * NLON))
    grad = ring_gather(ring_gather(grad, "y"), "x")
    grad_mixing = jnp.transpose(grad.reshape(K, 32, C), (1, 0, 2))
    return grad_features, grad_mixing


def solution(mesh):
    fine = Mesh(mesh.devices.reshape(2, 4, 4, 4, 2), ("zh", "y", "x", "zl", "co"))
    rows = ("zh", "y", "x")
    return jax.shard_map(
        per_device,
        mesh=fine,
        in_specs=(
            P(rows, AZ_AX, None),
            P(rows, AZ_AX, None),
            P(),
            P(None, rows, None, None, AZ_AX),
            P(rows),
        ),
        out_specs=(P(rows, AZ_AX, None), P(AZ_AX, None, None)),
        check_vma=False,
    )
```

```python
import math

import jax
import jax.numpy as jnp
from jax import lax
from jax.experimental import pallas as pl
from jax.experimental.pallas import tpu as pltpu
from jax.sharding import Mesh
from jax.sharding import PartitionSpec as P

BF = jnp.bfloat16
F32 = jnp.float32

K = 9
BW = 9
C = 256
NLON = 1440
NM = 720
REACH = 8
GRP = 32
TM = 24
GM = 90
MB = 4

ROWS_AX = ("zh", "y")
MODE_AX = ("x", "zl", "co")
AZ_AX = ("zl", "co")


def mode_table():
    n = jnp.arange(NLON, dtype=jnp.int32)
    xq = jnp.arange(4, dtype=jnp.int32)
    g = jnp.arange(8, dtype=jnp.int32)
    first = (xq[:, None] * TM + g[None, :] * GM).reshape(32)
    t = jnp.arange(TM, dtype=jnp.int32)
    step = 2.0 * math.pi / NLON
    ang_a = (first[:, None] * n[None, :] % NLON).astype(F32) * step
    ang_b = (t[:, None] * n[None, :] % NLON).astype(F32) * step
    norm = 1.0 / math.sqrt(NLON)
    ca, sa = jnp.cos(ang_a) * norm, jnp.sin(ang_a) * norm
    cb, sb = jnp.cos(ang_b), jnp.sin(ang_b)
    ca, sa, cb, sb = lax.optimization_barrier((ca, sa, cb, sb))
    ca, sa = ca[:, None, :], sa[:, None, :]
    cb, sb = cb[None], sb[None]
    real = (xq[:, None, None] * TM + t[None, None, :] < GM) & (g[None, :, None] >= 0)
    real = real.reshape(32, TM)[:, :, None].astype(F32)
    table = jnp.stack(((ca * cb - sa * sb) * real, -(sa * cb + ca * sb) * real), axis=1)
    return table.astype(BF).reshape(32 * 2 * TM, NLON)


def shift(x, axis, by):
    length = lax.axis_size(axis)
    return lax.ppermute(x, axis, [(i, i + by) for i in range(length) if 0 <= i + by < length])


def ring_pieces(x, axis, dim=0):
    n = lax.axis_size(axis)
    me = lax.axis_index(axis)
    own = lax.dynamic_index_in_dim(x, me, dim, False)
    got = []
    for s in range(1, n):
        piece = lax.dynamic_index_in_dim(x, lax.rem(me + s, n), dim, False)
        got.append((s, lax.ppermute(piece, axis, [(i, (i + s) % n) for i in range(n)])))
    return own, got


def ring_exchange(x, axis):
    n = lax.axis_size(axis)
    me = lax.axis_index(axis)
    own, got = ring_pieces(x, axis)
    came = [piece for _, piece in got[::-1]] + [own]
    return lax.dynamic_slice_in_dim(jnp.stack(came + came[:-1]), n - 1 - me, n, 0)


def ring_sum(x, axis, dim=0):
    own, got = ring_pieces(x.astype(BF), axis, dim)
    total = own.astype(F32)
    for _, piece in got:
        total = total + piece.astype(F32)
    return total


def ring_gather(x, axis):
    n = lax.axis_size(axis)
    me = lax.axis_index(axis)
    came = []
    for s in range(n - 1, 0, -1):
        came.append(lax.ppermute(x, axis, [(i, (i + s) % n) for i in range(n)]))
    came.append(x)
    return lax.dynamic_slice_in_dim(jnp.stack(came + came[:-1]), n - 1 - me, n, 0)


def band_matrices(response, offsets):
    first = (lax.axis_index("zh") * 4 + lax.axis_index("y")) * GRP + lax.axis_index("x") * 8
    rel = (offsets - first - jnp.arange(8, dtype=jnp.int32)).astype(BF)
    flat = jnp.transpose(response, (4, 1, 0, 2, 3)).reshape(GM, 8, K * BW * 2)
    flat = jnp.pad(flat, ((0, 4 * TM - GM), (0, 0), (0, 0)))
    flat = jnp.concatenate((flat, jnp.broadcast_to(rel[None, :, None], (4 * TM, 8, 1))), axis=2)
    wide = K * BW * 2 + 1
    parts = ring_exchange(flat.reshape(4, TM, 8 * wide), "x")
    low = shift(parts[3], ROWS_AX, 1)
    high = shift(parts[0], ROWS_AX, -1)
    parts = parts.reshape(4, TM, 8, wide)
    own = jnp.transpose(parts, (1, 3, 0, 2)).reshape(TM, wide, GRP)
    halo = jnp.transpose(jnp.stack((low, high), 0).reshape(2, TM, 8, wide), (1, 3, 0, 2))
    halo = halo.reshape(TM, wide, 2 * REACH)

    def columns(v):
        resp = v[:, :-1].astype(F32).reshape(TM, K, BW, 2, v.shape[2])
        a, b = resp[:, :, :, 0], resp[:, :, :, 1]
        return jnp.stack((jnp.concatenate((a, b), -1), jnp.concatenate((-b, a), -1)), 3)

    value = jnp.concatenate((columns(own), columns(halo)), -1)
    place_own = own[0, -1].astype(jnp.int32) + jnp.arange(GRP, dtype=jnp.int32)
    rim = jnp.arange(REACH, dtype=jnp.int32)
    place_halo = halo[0, -1].astype(jnp.int32) + jnp.concatenate((rim - REACH, rim + GRP))
    place = jnp.concatenate((place_own, place_own, place_halo, place_halo))
    which = jnp.arange(GRP, dtype=jnp.int32)[:, None] - place[None, :]
    value = lax.optimization_barrier(value)
    dense = jnp.zeros((TM, K, 2, GRP, 96), F32)
    for j in range(BW):
        dense = jnp.where(which == j, value[:, :, j, :, None, :], dense)
    return dense.astype(BF).reshape(TM, K * 2 * GRP, 96)


def dual_kernel(band_ref, own_ref, halo_ref, mix_ref, z_ref, dual_ref, column_ref):
    for m in range(MB):
        column_ref[0:64, :] = own_ref[m]
        column_ref[64:96, :] = halo_ref[m]
        z = jnp.dot(band_ref[m], column_ref[...], preferred_element_type=F32).astype(BF)
        for k in range(K):
            z_ref[k, m] = z[k * 64 : (k + 1) * 64]
    total = jnp.zeros((MB * 64, C), F32)
    for k in range(K):
        total = total + jnp.dot(
            z_ref[k].reshape(MB * 64, C), mix_ref[k], preferred_element_type=F32
        )
    dual_ref[...] = total.astype(BF).reshape(MB, 64, C)


def dual_call(band, own, halo, mix):
    return pl.pallas_call(
        dual_kernel,
        grid=(TM // MB,),
        in_specs=[
            pl.BlockSpec((MB, K * 64, 96), lambda i: (i, 0, 0)),
            pl.BlockSpec((MB, 64, C), lambda i: (i, 0, 0)),
            pl.BlockSpec((MB, 32, C), lambda i: (i, 0, 0)),
            pl.BlockSpec((K, C, C), lambda i: (0, 0, 0)),
        ],
        out_specs=[
            pl.BlockSpec((K, MB, 64, C), lambda i: (0, i, 0, 0)),
            pl.BlockSpec((MB, 64, C), lambda i: (i, 0, 0)),
        ],
        out_shape=[
            jax.ShapeDtypeStruct((K, TM, 64, C), BF),
            jax.ShapeDtypeStruct((TM, 64, C), BF),
        ],
        scratch_shapes=[pltpu.VMEM((96, C), BF)],
        compiler_params=pltpu.CompilerParams(vmem_limit_bytes=40 * 1024 * 1024),
        cost_estimate=pl.CostEstimate(
            flops=2 * TM * 576 * C * 96 + 2 * TM * 64 * K * C * C,
            bytes_accessed=16_000_000,
            transcendentals=0,
        ),
    )(band, own, halo, mix)


def grad_kernel(spec_ref, z_ref, out_ref, turned_ref):
    @pl.when(pl.program_id(0) == 0)
    def _():
        turned_ref[...] = spec_ref[...].T

    product = jnp.dot(turned_ref[...], z_ref[0], preferred_element_type=F32)
    turned = product.T.astype(BF)
    for g in range(8):
        out_ref[g % 2, g // 2, 0] = turned[g * 32 : (g + 1) * 32]


def grad_call(spec, z):
    return pl.pallas_call(
        grad_kernel,
        grid=(K,),
        in_specs=[
            pl.BlockSpec((TM * 64, C), lambda k: (0, 0)),
            pl.BlockSpec((1, TM * 64, C), lambda k: (k, 0, 0)),
        ],
        out_specs=pl.BlockSpec((2, 4, 1, 32, C), lambda k: (0, 0, k, 0, 0)),
        out_shape=jax.ShapeDtypeStruct((2, 4, K, 32, C), BF),
        scratch_shapes=[pltpu.VMEM((C, TM * 64), BF)],
        compiler_params=pltpu.CompilerParams(vmem_limit_bytes=24 * 1024 * 1024),
        cost_estimate=pl.CostEstimate(
            flops=2 * TM * 64 * K * C * C, bytes_accessed=9_000_000, transcendentals=0
        ),
    )(spec, z)


def to_modes(spec):
    return lax.all_to_all(spec.reshape(32, 2 * TM, C), MODE_AX, 0, 0, tiled=True)


def by_mode(block):
    rows = block.shape[0]
    return jnp.transpose(block.reshape(rows, 2, TM, C), (2, 1, 0, 3))


def per_device(features, cotangent, mixing, response, offsets):
    cot_row = lax.all_to_all(cotangent, AZ_AX, 0, 0, tiled=True).reshape(NLON, C)
    table = mode_table()
    mix_basis = jnp.moveaxis(mixing, 1, 0)
    cot_row, response, offsets = lax.optimization_barrier((cot_row, response, offsets))
    band = band_matrices(response, offsets)
    feat_row = lax.all_to_all(features, AZ_AX, 0, 0, tiled=True).reshape(NLON, C)

    q = jnp.arange(32 * 2 * TM, dtype=jnp.int32)
    first_mode = (q // (2 * TM) == 0) & (q % TM == 0)
    weight = jnp.where(first_mode, 1.0, 2.0).astype(F32)[:, None]
    cospec = (jnp.dot(table, cot_row, preferred_element_type=F32) * weight).astype(BF)
    cospec = to_modes(cospec)
    low = shift(cospec[GRP - REACH :], ROWS_AX, 1)
    high = shift(cospec[:REACH], ROWS_AX, -1)
    own = by_mode(cospec).reshape(TM, 64, C)
    halo = by_mode(jnp.concatenate((low, high), 0)).reshape(TM, 32, C)

    spec = jnp.dot(table, feat_row, preferred_element_type=F32).astype(BF)
    spec = by_mode(to_modes(spec)).reshape(TM * 64, C)

    z, dual = dual_call(band, own, halo, mix_basis)

    dual = jnp.transpose(dual.reshape(TM, 2, GRP, C), (2, 1, 0, 3)).reshape(GRP, 2 * TM, C)
    dual_row = lax.all_to_all(dual, MODE_AX, 0, 0, tiled=True).reshape(32 * 2 * TM, C)
    grad = grad_call(spec, z.reshape(K, TM * 64, C)).reshape(2, 4, K * 32, C)
    grad = ring_sum(grad, "co").reshape(4, 4, 72, C)
    grad = ring_sum(grad, "x", 1).astype(BF)
    grad, dual_row = lax.optimization_barrier((grad, dual_row))
    cells = lax.dot_general(
        table, dual_row, (((0,), (0,)), ((), ())), preferred_element_type=F32
    ).astype(BF)
    cells = cells.reshape(8, NLON // 8, C)

    grad = jnp.transpose(grad.reshape(4, 4, 18, C), (1, 0, 2, 3)).reshape(16, 18, C)
    grad = lax.all_to_all(grad, ("y", "zl"), 0, 0, tiled=True)
    grad, cells = lax.optimization_barrier((grad, cells))
    grad = jnp.sum(grad.astype(F32), 0)
    grad = grad + lax.ppermute(grad, "zh", [(0, 1), (1, 0)])
    grad, cells = lax.optimization_barrier((grad, cells))
    grad_features = lax.all_to_all(cells, AZ_AX, 0, 0, tiled=True)
    grad = grad * (1.0 / math.sqrt(256 * NLON))
    grad = lax.all_gather(grad, ("y", "x"), axis=0, tiled=False).reshape(4, 4, 18, C)
    grad = jnp.transpose(grad, (1, 0, 2, 3))
    grad_mixing = jnp.transpose(grad.reshape(K, 32, C), (1, 0, 2))
    return grad_features, grad_mixing


def solution(mesh):
    fine = Mesh(mesh.devices.reshape(2, 4, 4, 4, 2), ("zh", "y", "x", "zl", "co"))
    rows = ("zh", "y", "x")
    return jax.shard_map(
        per_device,
        mesh=fine,
        in_specs=(
            P(rows, AZ_AX, None),
            P(rows, AZ_AX, None),
            P(),
            P(None, rows, None, None, AZ_AX),
            P(rows),
        ),
        out_specs=(P(rows, AZ_AX, None), P(AZ_AX, None, None)),
        check_vma=False,
    )
```

```python
import math

import jax
import jax.numpy as jnp
from jax import lax
from jax.experimental import pallas as pl
from jax.experimental.pallas import tpu as pltpu
from jax.sharding import Mesh
from jax.sharding import PartitionSpec as P

BF = jnp.bfloat16
F32 = jnp.float32

K = 9
BW = 9
C = 256
NLON = 1440
NM = 720
REACH = 8
GRP = 32
TM = 24
GM = 90
MB = 4

ROWS_AX = ("zh", "y")
MODE_AX = ("x", "zl", "co")
AZ_AX = ("zl", "co")


def mode_table():
    n = jnp.arange(NLON, dtype=jnp.int32)
    xq = jnp.arange(4, dtype=jnp.int32)
    g = jnp.arange(8, dtype=jnp.int32)
    first = (xq[:, None] * TM + g[None, :] * GM).reshape(32)
    t = jnp.arange(TM, dtype=jnp.int32)
    step = 2.0 * math.pi / NLON
    ang_a = (first[:, None] * n[None, :] % NLON).astype(F32) * step
    ang_b = (t[:, None] * n[None, :] % NLON).astype(F32) * step
    norm = 1.0 / math.sqrt(NLON)
    ca, sa = jnp.cos(ang_a) * norm, jnp.sin(ang_a) * norm
    cb, sb = jnp.cos(ang_b), jnp.sin(ang_b)
    ca, sa, cb, sb = lax.optimization_barrier((ca, sa, cb, sb))
    ca, sa = ca[:, None, :], sa[:, None, :]
    cb, sb = cb[None], sb[None]
    real = (xq[:, None, None] * TM + t[None, None, :] < GM) & (g[None, :, None] >= 0)
    real = real.reshape(32, TM)[:, :, None].astype(F32)
    table = jnp.stack(((ca * cb - sa * sb) * real, -(sa * cb + ca * sb) * real), axis=1)
    return table.astype(BF).reshape(32 * 2 * TM, NLON)


def shift(x, axis, by):
    length = lax.axis_size(axis)
    return lax.ppermute(x, axis, [(i, i + by) for i in range(length) if 0 <= i + by < length])


def ring_pieces(x, axis, dim=0):
    n = lax.axis_size(axis)
    me = lax.axis_index(axis)
    own = lax.dynamic_index_in_dim(x, me, dim, False)
    got = []
    for s in range(1, n):
        piece = lax.dynamic_index_in_dim(x, lax.rem(me + s, n), dim, False)
        got.append((s, lax.ppermute(piece, axis, [(i, (i + s) % n) for i in range(n)])))
    return own, got


def ring_exchange(x, axis):
    n = lax.axis_size(axis)
    me = lax.axis_index(axis)
    own, got = ring_pieces(x, axis)
    came = [piece for _, piece in got[::-1]] + [own]
    return lax.dynamic_slice_in_dim(jnp.stack(came + came[:-1]), n - 1 - me, n, 0)


def ring_sum(x, axis, dim=0):
    own, got = ring_pieces(x.astype(BF), axis, dim)
    total = own.astype(F32)
    for _, piece in got:
        total = total + piece.astype(F32)
    return total


def ring_gather(x, axis):
    n = lax.axis_size(axis)
    me = lax.axis_index(axis)
    came = []
    for s in range(n - 1, 0, -1):
        came.append(lax.ppermute(x, axis, [(i, (i + s) % n) for i in range(n)]))
    came.append(x)
    return lax.dynamic_slice_in_dim(jnp.stack(came + came[:-1]), n - 1 - me, n, 0)


def band_matrices(response, offsets):
    first = (lax.axis_index("zh") * 4 + lax.axis_index("y")) * GRP + lax.axis_index("x") * 8
    rel = (offsets - first - jnp.arange(8, dtype=jnp.int32)).astype(BF)
    flat = jnp.transpose(response, (4, 1, 0, 2, 3)).reshape(GM, 8, K * BW * 2)
    flat = jnp.pad(flat, ((0, 4 * TM - GM), (0, 0), (0, 0)))
    flat = jnp.concatenate((flat, jnp.broadcast_to(rel[None, :, None], (4 * TM, 8, 1))), axis=2)
    wide = K * BW * 2 + 1
    parts = ring_exchange(flat.reshape(4, TM, 8 * wide), "x")
    low = shift(parts[3], ROWS_AX, 1)
    high = shift(parts[0], ROWS_AX, -1)
    parts = parts.reshape(4, TM, 8, wide)
    own = jnp.transpose(parts, (1, 3, 0, 2)).reshape(TM, wide, GRP)
    halo = jnp.transpose(jnp.stack((low, high), 0).reshape(2, TM, 8, wide), (1, 3, 0, 2))
    halo = halo.reshape(TM, wide, 2 * REACH)

    def columns(v):
        resp = v[:, :-1].astype(F32).reshape(TM, K, BW, 2, v.shape[2])
        a, b = resp[:, :, :, 0], resp[:, :, :, 1]
        return jnp.stack((jnp.concatenate((a, b), -1), jnp.concatenate((-b, a), -1)), 3)

    value = jnp.concatenate((columns(own), columns(halo)), -1)
    place_own = own[0, -1].astype(jnp.int32) + jnp.arange(GRP, dtype=jnp.int32)
    rim = jnp.arange(REACH, dtype=jnp.int32)
    place_halo = halo[0, -1].astype(jnp.int32) + jnp.concatenate((rim - REACH, rim + GRP))
    place = jnp.concatenate((place_own, place_own, place_halo, place_halo))
    which = jnp.arange(GRP, dtype=jnp.int32)[:, None] - place[None, :]
    value = lax.optimization_barrier(value)
    dense = jnp.zeros((TM, K, 2, GRP, 96), F32)
    for j in range(BW):
        dense = jnp.where(which == j, value[:, :, j, :, None, :], dense)
    return dense.astype(BF).reshape(TM, K * 2 * GRP, 96)


def dual_kernel(band_ref, own_ref, halo_ref, mix_ref, z_ref, dual_ref, column_ref):
    for m in range(MB):
        column_ref[0:64, :] = own_ref[m]
        column_ref[64:96, :] = halo_ref[m]
        z = jnp.dot(band_ref[m], column_ref[...], preferred_element_type=F32).astype(BF)
        for k in range(K):
            z_ref[k, m] = z[k * 64 : (k + 1) * 64]
    total = jnp.zeros((MB * 64, C), F32)
    for k in range(K):
        total = total + jnp.dot(
            z_ref[k].reshape(MB * 64, C), mix_ref[k], preferred_element_type=F32
        )
    dual_ref[...] = total.astype(BF).reshape(MB, 64, C)


def dual_call(band, own, halo, mix):
    return pl.pallas_call(
        dual_kernel,
        grid=(TM // MB,),
        in_specs=[
            pl.BlockSpec((MB, K * 64, 96), lambda i: (i, 0, 0)),
            pl.BlockSpec((MB, 64, C), lambda i: (i, 0, 0)),
            pl.BlockSpec((MB, 32, C), lambda i: (i, 0, 0)),
            pl.BlockSpec((K, C, C), lambda i: (0, 0, 0)),
        ],
        out_specs=[
            pl.BlockSpec((K, MB, 64, C), lambda i: (0, i, 0, 0)),
            pl.BlockSpec((MB, 64, C), lambda i: (i, 0, 0)),
        ],
        out_shape=[
            jax.ShapeDtypeStruct((K, TM, 64, C), BF),
            jax.ShapeDtypeStruct((TM, 64, C), BF),
        ],
        scratch_shapes=[pltpu.VMEM((96, C), BF)],
        compiler_params=pltpu.CompilerParams(vmem_limit_bytes=40 * 1024 * 1024),
        cost_estimate=pl.CostEstimate(
            flops=2 * TM * 576 * C * 96 + 2 * TM * 64 * K * C * C,
            bytes_accessed=16_000_000,
            transcendentals=0,
        ),
    )(band, own, halo, mix)


def grad_kernel(spec_ref, z_ref, out_ref, turned_ref):
    @pl.when(pl.program_id(0) == 0)
    def _():
        turned_ref[...] = spec_ref[...].T

    product = jnp.dot(turned_ref[...], z_ref[0], preferred_element_type=F32)
    turned = product.T.astype(BF)
    for g in range(8):
        out_ref[g % 2, g // 2, 0] = turned[g * 32 : (g + 1) * 32]


def grad_call(spec, z):
    return pl.pallas_call(
        grad_kernel,
        grid=(K,),
        in_specs=[
            pl.BlockSpec((TM * 64, C), lambda k: (0, 0)),
            pl.BlockSpec((1, TM * 64, C), lambda k: (k, 0, 0)),
        ],
        out_specs=pl.BlockSpec((2, 4, 1, 32, C), lambda k: (0, 0, k, 0, 0)),
        out_shape=jax.ShapeDtypeStruct((2, 4, K, 32, C), BF),
        scratch_shapes=[pltpu.VMEM((C, TM * 64), BF)],
        compiler_params=pltpu.CompilerParams(vmem_limit_bytes=24 * 1024 * 1024),
        cost_estimate=pl.CostEstimate(
            flops=2 * TM * 64 * K * C * C, bytes_accessed=9_000_000, transcendentals=0
        ),
    )(spec, z)


def to_modes(spec):
    return lax.all_to_all(spec.reshape(32, 2 * TM, C), MODE_AX, 0, 0, tiled=True)


def by_mode(block):
    rows = block.shape[0]
    return jnp.transpose(block.reshape(rows, 2, TM, C), (2, 1, 0, 3))


def per_device(features, cotangent, mixing, response, offsets):
    cot_row = lax.all_to_all(cotangent, AZ_AX, 0, 0, tiled=True).reshape(NLON, C)
    table = mode_table()
    mix_basis = jnp.moveaxis(mixing, 1, 0)
    cot_row, response, offsets = lax.optimization_barrier((cot_row, response, offsets))
    band = band_matrices(response, offsets)
    feat_row = lax.all_to_all(features, AZ_AX, 0, 0, tiled=True).reshape(NLON, C)

    q = jnp.arange(32 * 2 * TM, dtype=jnp.int32)
    first_mode = (q // (2 * TM) == 0) & (q % TM == 0)
    weight = jnp.where(first_mode, 1.0, 2.0).astype(F32)[:, None]
    cospec = (jnp.dot(table, cot_row, preferred_element_type=F32) * weight).astype(BF)
    cospec = to_modes(cospec)
    low = shift(cospec[GRP - REACH :], ROWS_AX, 1)
    high = shift(cospec[:REACH], ROWS_AX, -1)
    own = by_mode(cospec).reshape(TM, 64, C)
    halo = by_mode(jnp.concatenate((low, high), 0)).reshape(TM, 32, C)

    spec = jnp.dot(table, feat_row, preferred_element_type=F32).astype(BF)
    spec = by_mode(to_modes(spec)).reshape(TM * 64, C)

    z, dual = dual_call(band, own, halo, mix_basis)

    dual = jnp.transpose(dual.reshape(TM, 2, GRP, C), (2, 1, 0, 3)).reshape(GRP, 2 * TM, C)
    dual_row = lax.all_to_all(dual, MODE_AX, 0, 0, tiled=True).reshape(32 * 2 * TM, C)
    grad = grad_call(spec, z.reshape(K, TM * 64, C)).reshape(2, 4, K * 32, C)
    grad = ring_sum(grad, "co").reshape(4, 4, 72, C)
    grad = ring_sum(grad, "x", 1).astype(BF)
    grad, dual_row = lax.optimization_barrier((grad, dual_row))
    cells = lax.dot_general(
        table, dual_row, (((0,), (0,)), ((), ())), preferred_element_type=F32
    ).astype(BF)
    cells = cells.reshape(8, NLON // 8, C)

    grad = jnp.transpose(grad.reshape(4, 4, 18, C), (1, 0, 2, 3))[None]
    grad = jnp.broadcast_to(grad, (2, 4, 4, 18, C)).reshape(32, 18, C)
    grad = lax.all_to_all(grad, ("zh", "y", "zl"), 0, 0, tiled=True)
    grad, cells = lax.optimization_barrier((grad, cells))
    grad = jnp.sum(grad.astype(F32), 0)
    grad_features = lax.all_to_all(cells, AZ_AX, 0, 0, tiled=True)
    grad = grad * (1.0 / math.sqrt(256 * NLON))
    grad = lax.all_gather(grad, ("y", "x"), axis=0, tiled=False).reshape(4, 4, 18, C)
    grad = jnp.transpose(grad, (1, 0, 2, 3))
    grad_mixing = jnp.transpose(grad.reshape(K, 32, C), (1, 0, 2))
    return grad_features, grad_mixing


def solution(mesh):
    fine = Mesh(mesh.devices.reshape(2, 4, 4, 4, 2), ("zh", "y", "x", "zl", "co"))
    rows = ("zh", "y", "x")
    return jax.shard_map(
        per_device,
        mesh=fine,
        in_specs=(
            P(rows, AZ_AX, None),
            P(rows, AZ_AX, None),
            P(),
            P(None, rows, None, None, AZ_AX),
            P(rows),
        ),
        out_specs=(P(rows, AZ_AX, None), P(AZ_AX, None, None)),
        check_vma=False,
    )
```
